512 devices in a mesh: axial: 128 (over z_lo, y, x, core), batch: 4 (over z_hi).
Axes of the slice: x: 4, y: 8, z: 8 (z_hi: 4, z_lo: 2; z = z_hi * 2 + z_lo), core: 2. Of those that a mesh axis runs over, the one named last changes fastest.
Arguments:
- pair: bfloat16 [1024, 256, 128], P(('batch', 'axial')), parts along dimension 0, may hold values from -6 to 6
- residue_mask: int32 [1024], P(('batch', 'axial')), parts along dimension 0, may hold values 0 or 1
- gate_left: bfloat16 [128, 128], replicated, may hold values from -0.5 to 0.5
- proj_left: bfloat16 [128, 128], replicated, may hold values from -0.5 to 0.5
- gate_right: bfloat16 [128, 128], replicated, may hold values from -0.5 to 0.5
- proj_right: bfloat16 [128, 128], replicated, may hold values from -0.5 to 0.5
- gate_out: bfloat16 [128, 128], replicated, may hold values from -0.5 to 0.5
- proj_out: bfloat16 [128, 128], replicated, may hold values from -0.5 to 0.5
Outputs:
- updated: bfloat16 [1024, 256, 128], P('batch', 'axial'), parts along dimension 0
The draws below stay inside these ranges and needn't reach their ends.
There are 4 independent parts, one for each index of `batch`. The reference program is written for one: setup_inputs(seed, part) draws one part's arguments, and reference() takes and returns one part's arrays. A program takes and returns all parts, laid end to end along the dimension named above; an argument that names none is the same for every part. Nothing has to cross between parts.
All inputs are finite; a program needn't handle non-finite values. No bound on the sum of `residue_mask` on one device may be relied on, other than what follows from the above.
Results may differ from the reference program's by a relative error of at most 0.004.
Values may be sent and summed in bfloat16 or wider, within the bound.
A program may use at most 64 MiB of HBM per device.

```python
import jax
import jax.numpy as jnp
from jax import lax

CZ = 128
CH = 128
ROWS_DEV = 2
N = 256
N_AXIAL = 128


def place_ends(values, rng, smallest, largest):
    dims = values.shape
    index_at = [jax.random.randint(jax.random.fold_in(rng, axis), (), 0, dims[axis]) for axis in range(len(dims))]
    values = values.at[tuple(index_at)].set(smallest)
    longest = dims.index(max(dims))
    index_at[longest] = (index_at[longest] + 1) % dims[longest]
    return values.at[tuple(index_at)].set(largest)


def block_levels(own_key, dims, split, low, high):
    factor_of, own = 1.0, jax.random.fold_in(own_key, 6)
    for position, shards_of in split:
        steps = jnp.exp(jax.random.uniform(jax.random.fold_in(own, position), (shards_of,), jnp.float32, low / len(split), high / len(split)))
        factor_of = factor_of * jnp.repeat(steps, dims[position] // shards_of).reshape([-1 if axis == position else 1 for axis in range(len(dims))])
    return factor_of


def gaussian(rng, shape, width, bound, shards=(), kind=jnp.bfloat16):
    entries = jax.random.normal(rng, shape, jnp.float32) * width
    if len(shards) > 0:
        entries = block_levels(rng, shape, shards, -0.22, 0.18) * entries
    return jnp.clip(entries, min=-bound, max=bound).astype(kind)


def setup_inputs(seed: int = 0, part: int = 0) -> dict:
    arg_keys = jax.random.split(jax.random.key(seed), 9)
    part_splits = jax.random.split(jax.random.fold_in(arg_keys[8], part), 9)
    pair = gaussian(part_splits[0], (N, N, CZ), 1.0, 6.0, ((0, 128),))
    residue_mask = place_ends((jax.random.randint(part_splits[1], (N,), 0, 4) < 3).astype(jnp.int32), jax.random.fold_in(part_splits[1], 1), 0, 1)
    gate_left = gaussian(arg_keys[2], (CZ, CH), CZ ** -0.5, 0.5)
    proj_left = gaussian(arg_keys[3], (CZ, CH), CZ ** -0.5, 0.5)
    gate_right = gaussian(arg_keys[4], (CZ, CH), CZ ** -0.5, 0.5)
    proj_right = gaussian(arg_keys[5], (CZ, CH), CZ ** -0.5, 0.5)
    gate_out = gaussian(arg_keys[6], (CZ, CZ), CZ ** -0.5, 0.5)
    proj_out = gaussian(arg_keys[7], (CH, CZ), CH ** -0.5, 0.5)
    return {"pair": pair, "residue_mask": residue_mask, "gate_left": gate_left, "proj_left": proj_left, "gate_right": gate_right, "proj_right": proj_right, "gate_out": gate_out, "proj_out": proj_out}


def layer_norm(values, axis):
    mean = lax.optimization_barrier(jnp.mean(values, axis=axis, keepdims=True))
    centered = values - mean
    var = lax.optimization_barrier(jnp.mean(centered * centered, axis=axis, keepdims=True))
    return centered / jnp.sqrt(var + 1e-05)

def reference(pair, residue_mask, gate_left, proj_left, gate_right, proj_right, gate_out, proj_out):
    weights = residue_mask.astype(jnp.float32)
    blocks = pair.reshape(N_AXIAL, ROWS_DEV, N, CZ)
    mask_blocks = weights.reshape(N_AXIAL, ROWS_DEV)

    def factor(normed_wide, pair_mask, gate_w, proj_w):
        gating = jnp.einsum('ikc,ch->hik', normed_wide, gate_w.astype(jnp.float32))
        values = jnp.einsum('ikc,ch->hik', normed_wide, proj_w.astype(jnp.float32))
        return (jax.nn.sigmoid(gating) * values * pair_mask[None]).astype(jnp.bfloat16)

    def make_factors(inputs):
        block, mask_rows = inputs
        normed_wide = layer_norm(block.astype(jnp.float32), 2).astype(jnp.bfloat16).astype(jnp.float32)
        pair_mask = mask_rows[:, None] * weights[None, :]
        return (factor(normed_wide, pair_mask, gate_left, proj_left), factor(normed_wide, pair_mask, gate_right, proj_right))
    left, right = lax.map(make_factors, (blocks, mask_blocks))
    left = jnp.transpose(left, (1, 0, 2, 3)).reshape(CH, N, N)
    right = jnp.transpose(right, (1, 0, 2, 3)).reshape(CH, N, N)

    def channel_product(inputs):
        left_h, right_h = inputs
        return jnp.dot(left_h, right_h.T, preferred_element_type=jnp.float32).astype(jnp.bfloat16)
    products = lax.map(channel_product, (left, right))
    prod_blocks = jnp.transpose(products.reshape(CH, N_AXIAL, ROWS_DEV, N), (1, 0, 2, 3))

    def finish(inputs):
        block, prod_block = inputs
        normed_wide = layer_norm(block.astype(jnp.float32), 2).astype(jnp.bfloat16).astype(jnp.float32)
        prod_normed = layer_norm(prod_block.astype(jnp.float32), 0).astype(jnp.bfloat16)
        update = jnp.einsum('hij,hc->ijc', prod_normed.astype(jnp.float32), proj_out.astype(jnp.float32))
        gating = jax.nn.sigmoid(jnp.einsum('ijc,cd->ijd', normed_wide, gate_out.astype(jnp.float32)))
        return (block.astype(jnp.float32) + gating * update).astype(jnp.bfloat16)
    result = lax.map(finish, (blocks, prod_blocks))
    return result.reshape(N, N, CZ)
```

```python
import itertools

import jax
import jax.numpy as jnp
from jax import lax
from jax.experimental import pallas as pl
from jax.experimental.pallas import tpu as pltpu
from jax.sharding import PartitionSpec as P

MESH = pl.DeviceIdType.MESH
F32, BF16 = jnp.float32, jnp.bfloat16
NZ, NY, NX, NC = 2, 8, 4, 2
D = NZ * NY * NX * NC
CH = 128
Y_ORDER = (4, 3, 5, 2, 6, 1, 7, 0)
X_ORDER = (2, 1, 3, 0)
PEERS = tuple(
    (dz, dy, dx, dc)
    for dy, dx, dz, dc in itertools.product(Y_ORDER, X_ORDER, (1, 0), (0, 1))
    if dz + dy + dx + dc
)
NT = (((1,), (1,)), ((), ()))
TN = (((0,), (0,)), ((), ()))


def layer_norm(values, axis):
    mean = jnp.mean(values, axis=axis, keepdims=True)
    centered = values - mean
    var = jnp.mean(centered * centered, axis=axis, keepdims=True)
    return centered * lax.rsqrt(var + 1e-05)


def kernel(
    pair_hbm, mask_ref, gl_hbm, pl_hbm, gr_hbm, pr_hbm, go_hbm, po_hbm, out_ref,
    pair_v, w_v, msg, fac, prod, prods, pairs, mx, my, mz, mask_v, s8, s4, gate_v,
    load_sem, wload_sem, send_sem, fac_sem, prods_sem, pairs_sem, mask_sem,
):
    me = lax.axis_index("axial")
    z, y = lax.div(me, 64), lax.rem(lax.div(me, 8), 8)
    x, c = lax.rem(lax.div(me, 2), 4), lax.rem(me, 2)
    zt = [64 * lax.rem(z + k, 2) for k in range(NZ)]
    yt = [8 * lax.rem(y + k, 8) for k in range(NY)]
    xt = [2 * lax.rem(x + k, 4) for k in range(NX)]
    ct = [lax.rem(c + k, 2) for k in range(NC)]
    targets = [zt[dz] + yt[dy] + xt[dx] + ct[dc] for dz, dy, dx, dc in PEERS]

    load = pltpu.make_async_copy(pair_hbm, pair_v, load_sem)
    load.start()
    wloads = [
        pltpu.make_async_copy(ref, w_v.at[i], wload_sem.at[i])
        for i, ref in enumerate((gl_hbm, pl_hbm, gr_hbm, pr_hbm, go_hbm, po_hbm))
    ]
    for w in wloads:
        w.start()
    barrier = pltpu.get_barrier_semaphore()
    for t in targets:
        pl.semaphore_signal(barrier, inc=1, device_id={"axial": t}, device_id_type=MESH)

    def send(src, dst, sem, recv_sem, t):
        pltpu.make_async_remote_copy(
            src_ref=src, dst_ref=dst, send_sem=sem, recv_sem=recv_sem,
            device_id={"axial": t}, device_id_type=MESH,
        ).start()

    def landed(ref, sem):
        pltpu.make_async_copy(ref, ref, sem).wait()

    load.wait()
    normed = layer_norm(pair_v.reshape(512, 128)[...].astype(F32), 1).astype(BF16)
    for w in wloads:
        w.wait()
    for f in range(2):
        gating = lax.dot_general(
            w_v[2 * f], normed, (((0,), (1,)), ((), ())), preferred_element_type=F32
        )
        values = lax.dot_general(
            w_v[2 * f + 1], normed, (((0,), (1,)), ((), ())), preferred_element_type=F32
        )
        factor = jax.nn.sigmoid(gating) * values
        for r in range(2):
            row_mask = mask_ref[r].astype(F32)
            for kh in range(2):
                q = 2 * r + kh
                s8[pl.ds(4 * f + q, 128, stride=8), :] = (
                    factor[:, 128 * q : 128 * q + 128] * row_mask
                )
    msg.reshape(1024, 128)[...] = s8[...].astype(BF16)

    k_index = lax.broadcasted_iota(jnp.int32, (2, 128), 0) * 128 + lax.broadcasted_iota(
        jnp.int32, (2, 128), 1
    )
    own_mask = jnp.where(k_index == 2 * me, mask_ref[0], 0) + jnp.where(
        k_index == 2 * me + 1, mask_ref[1], 0
    )
    xc = 2 * x + c
    mx[xc] = own_mask.astype(F32)

    pl.semaphore_wait(barrier, D - 1)

    for dx, dc in itertools.product(range(NX), range(NC)):
        if dx + dc:
            send(mx.at[xc], mx.at[xc], mask_sem.at[0], mask_sem.at[1], zt[0] + yt[0] + xt[dx] + ct[dc])
    for t in targets:
        send(msg.at[t], fac.at[me], send_sem.at[0], fac_sem, t)
    pltpu.make_async_copy(msg.at[me], fac.at[me], fac_sem).start()

    landed(mx.at[pl.ds(0, 7)], mask_sem.at[1])
    my[y] = jnp.sum(mx[...], axis=0)
    for dy in range(1, NY):
        send(my.at[y], my.at[y], mask_sem.at[2], mask_sem.at[3], zt[0] + yt[dy] + xt[0] + ct[0])
    for t in targets:
        send(pair_v.at[:, t], pairs.at[me], send_sem.at[1], pairs_sem, t)
    pltpu.make_async_copy(pair_v.at[:, me], pairs.at[me], pairs_sem).start()
    landed(my.at[pl.ds(0, 7)], mask_sem.at[3])
    mz[z] = jnp.sum(my[...], axis=0)
    send(mz.at[z], mz.at[z], mask_sem.at[4], mask_sem.at[5], zt[1] + yt[0] + xt[0] + ct[0])
    landed(mz.at[pl.ds(0, 1)], mask_sem.at[5])
    mask_v[...] = jnp.sum(mz[...], axis=0)

    landed(fac, fac_sem)
    s8[...] = fac.reshape(1024, 128)[...].astype(F32)
    halves = [s8[pl.ds(q, 128, stride=8), :] for q in range(8)]
    lefts = [
        jnp.concatenate(
            [halves[2 * r + kh] * mask_v[kh : kh + 1, :] for kh in range(2)], axis=1
        )
        for r in range(2)
    ]
    left = jnp.concatenate(lefts, axis=0).astype(BF16)
    rights = [jnp.concatenate(halves[4 + 2 * r : 6 + 2 * r], axis=1) for r in range(2)]
    right = jnp.concatenate(rights, axis=0).astype(BF16)
    product = lax.dot_general(right, left, NT, preferred_element_type=F32)
    for rj, ri in itertools.product(range(2), range(2)):
        s4[pl.ds(2 * rj + ri, 128, stride=4), :] = product[
            128 * rj : 128 * rj + 128, 128 * ri : 128 * ri + 128
        ]
    prod.reshape(512, 128)[...] = s4[...].astype(BF16)
    for t in targets:
        send(prod.at[t], prods.at[me], send_sem.at[2], prods_sem, t)
    pltpu.make_async_copy(prod.at[me], prods.at[me], prods_sem).start()

    landed(pairs, pairs_sem)
    columns = pairs.reshape(512, 128)
    normed = layer_norm(columns[...].astype(F32), 1).astype(BF16)
    gate_v[...] = jax.nn.sigmoid(
        jnp.dot(normed, w_v[4], preferred_element_type=F32)
    )

    landed(prods, prods_sem)
    s4[...] = prods.reshape(512, 128)[...].astype(F32)
    update = []
    for rj, ri in itertools.product(range(2), range(2)):
        channels = s4[pl.ds(2 * rj + ri, 128, stride=4), :]
        update.append(
            lax.dot_general(
                layer_norm(channels, 0).astype(BF16), w_v[5], TN, preferred_element_type=F32
            )
        )
    for (rj, ri), part in zip(itertools.product(range(2), range(2)), update):
        s4[pl.ds(2 * ri + rj, 128, stride=4), :] = part
    out_ref[...] = (columns[...].astype(F32) + gate_v[...] * s4[...]).astype(BF16)

    landed(msg.at[pl.ds(0, D - 1)], send_sem.at[0])
    landed(pairs.at[pl.ds(0, D - 1)], send_sem.at[1])
    landed(prod.at[pl.ds(0, D - 1)], send_sem.at[2])
    landed(mx.at[pl.ds(0, 7)], mask_sem.at[0])
    landed(my.at[pl.ds(0, 7)], mask_sem.at[2])
    landed(mz.at[pl.ds(0, 1)], mask_sem.at[4])


def body(pair, residue_mask, *weights):
    hbm = pl.BlockSpec(memory_space=pltpu.HBM)
    out = pl.pallas_call(
        kernel,
        out_shape=jax.ShapeDtypeStruct((512, 128), BF16),
        in_specs=[hbm, pl.BlockSpec(memory_space=pltpu.SMEM)] + [hbm] * 6,
        out_specs=pl.BlockSpec(memory_space=pltpu.VMEM),
        scratch_shapes=[
            pltpu.VMEM((2, D, 2, 128), BF16),
            pltpu.VMEM((6, 128, 128), BF16),
            pltpu.VMEM((D, 8, 128), BF16),
            pltpu.VMEM((D, 8, 128), BF16),
            pltpu.VMEM((D, 4, 128), BF16),
            pltpu.VMEM((D, 4, 128), BF16),
            pltpu.VMEM((D, 2, 2, 128), BF16),
            pltpu.VMEM((8, 2, 128), F32),
            pltpu.VMEM((8, 2, 128), F32),
            pltpu.VMEM((2, 2, 128), F32),
            pltpu.VMEM((2, 128), F32),
            pltpu.VMEM((1024, 128), F32),
            pltpu.VMEM((512, 128), F32),
            pltpu.VMEM((512, 128), F32),
            pltpu.SemaphoreType.DMA,
            pltpu.SemaphoreType.DMA((6,)),
            pltpu.SemaphoreType.DMA((3,)),
            pltpu.SemaphoreType.DMA,
            pltpu.SemaphoreType.DMA,
            pltpu.SemaphoreType.DMA,
            pltpu.SemaphoreType.DMA((6,)),
        ],
        compiler_params=pltpu.CompilerParams(
            collective_id=0, has_side_effects=True, vmem_limit_bytes=60 << 20
        ),
    )(pair.reshape(2, D, 2, 128), residue_mask, *weights)
    return out.reshape(256, 2, 128)


def solution(mesh):
    return jax.shard_map(
        body,
        mesh=mesh,
        in_specs=(P(("batch", "axial"), None, None), P(("batch", "axial")))
        + (P(),) * 6,
        out_specs=P("batch", "axial", None),
        check_vma=False,
    )
```

```python
import itertools

import jax
import jax.numpy as jnp
from jax import lax
from jax.experimental import pallas as pl
from jax.experimental.pallas import tpu as pltpu
from jax.sharding import PartitionSpec as P

MESH = pl.DeviceIdType.MESH
F32, BF16 = jnp.float32, jnp.bfloat16
NZ, NY, NX, NC = 2, 8, 4, 2
D = NZ * NY * NX * NC
CH = 128
Y_ORDER = (4, 3, 5, 2, 6, 1, 7, 0)
X_ORDER = (2, 1, 3, 0)
PEERS = tuple(
    (dz, dy, dx, dc)
    for dy, dx, dz, dc in itertools.product(Y_ORDER, X_ORDER, (1, 0), (0, 1))
    if dz + dy + dx + dc
)
EARLY = 112
NT = (((1,), (1,)), ((), ()))
TN = (((0,), (0,)), ((), ()))


def layer_norm(values, axis):
    mean = jnp.mean(values, axis=axis, keepdims=True)
    centered = values - mean
    var = jnp.mean(centered * centered, axis=axis, keepdims=True)
    return centered * lax.rsqrt(var + 1e-05)


def kernel(
    pair_hbm, mask_ref, gl_hbm, pl_hbm, gr_hbm, pr_hbm, go_hbm, po_hbm, out_ref,
    pair_v, w_v, msg, fac, prod, prods, pairs, mx, my, mask_v, s8, s4, gate_v,
    load_sem, wload_sem, send_sem, fac_sem, prods_sem, pairs_sem, mask_sem,
):
    me = lax.axis_index("axial")
    z, y = lax.div(me, 64), lax.rem(lax.div(me, 8), 8)
    x, c = lax.rem(lax.div(me, 2), 4), lax.rem(me, 2)
    zt = [64 * lax.rem(z + k, 2) for k in range(NZ)]
    yt = [8 * lax.rem(y + k, 8) for k in range(NY)]
    xt = [2 * lax.rem(x + k, 4) for k in range(NX)]
    ct = [lax.rem(c + k, 2) for k in range(NC)]
    targets = [zt[dz] + yt[dy] + xt[dx] + ct[dc] for dz, dy, dx, dc in PEERS]

    barrier = pltpu.get_barrier_semaphore()
    for t in targets:
        pl.semaphore_signal(barrier, inc=1, device_id={"axial": t}, device_id_type=MESH)

    load = pltpu.make_async_copy(pair_hbm, pair_v, load_sem)
    load.start()
    wloads = [
        pltpu.make_async_copy(ref, w_v.at[i], wload_sem.at[i])
        for i, ref in enumerate((gl_hbm, pl_hbm, gr_hbm, pr_hbm, go_hbm, po_hbm))
    ]
    for w in wloads:
        w.start()

    def send(src, dst, sem, recv_sem, t):
        pltpu.make_async_remote_copy(
            src_ref=src, dst_ref=dst, send_sem=sem, recv_sem=recv_sem,
            device_id={"axial": t}, device_id_type=MESH,
        ).start()

    def landed(ref, sem):
        pltpu.make_async_copy(ref, ref, sem).wait()

    load.wait()
    normed = layer_norm(pair_v.reshape(512, 128)[...].astype(F32), 1).astype(BF16)
    for w in wloads:
        w.wait()
    for f in range(2):
        gating = lax.dot_general(
            w_v[2 * f], normed, (((0,), (1,)), ((), ())), preferred_element_type=F32
        )
        values = lax.dot_general(
            w_v[2 * f + 1], normed, (((0,), (1,)), ((), ())), preferred_element_type=F32
        )
        factor = jax.nn.sigmoid(gating) * values
        for r in range(2):
            row_mask = mask_ref[r].astype(F32)
            for kh in range(2):
                q = 2 * r + kh
                s8[pl.ds(4 * f + q, 128, stride=8), :] = (
                    factor[:, 128 * q : 128 * q + 128] * row_mask
                )
    msg.reshape(1024, 128)[...] = s8[...].astype(BF16)

    k_index = lax.broadcasted_iota(jnp.int32, (2, 128), 0) * 128 + lax.broadcasted_iota(
        jnp.int32, (2, 128), 1
    )
    own_mask = jnp.where(k_index == 2 * me, mask_ref[0], 0) + jnp.where(
        k_index == 2 * me + 1, mask_ref[1], 0
    )
    xc, zy = 2 * x + c, 8 * z + y
    mx[xc] = own_mask.astype(F32)

    pl.semaphore_wait(barrier, D - 1)

    for dx, dc in itertools.product(range(NX), range(NC)):
        if dx + dc:
            t = zt[0] + yt[0] + xt[dx] + ct[dc]
            send(mx.at[xc], mx.at[xc], mask_sem.at[0], mask_sem.at[1], t)
    for t in targets[:EARLY]:
        send(msg.at[t], fac.at[me], send_sem.at[0], fac_sem, t)
    landed(mx.at[pl.ds(0, 7)], mask_sem.at[1])
    my[zy] = jnp.sum(mx[...], axis=0)
    for dy, dz in itertools.product(Y_ORDER, (1, 0)):
        if dy + dz:
            t = zt[dz] + yt[dy] + xt[0] + ct[0]
            send(my.at[zy], my.at[zy], mask_sem.at[2], mask_sem.at[3], t)
    for t in targets[EARLY:]:
        send(msg.at[t], fac.at[me], send_sem.at[0], fac_sem, t)
    pltpu.make_async_copy(msg.at[me], fac.at[me], fac_sem).start()
    for t in targets:
        send(pair_v.at[:, t], pairs.at[me], send_sem.at[1], pairs_sem, t)
    pltpu.make_async_copy(pair_v.at[:, me], pairs.at[me], pairs_sem).start()
    landed(my.at[pl.ds(0, 15)], mask_sem.at[3])
    mask_v[...] = jnp.sum(my[...], axis=0)

    landed(fac, fac_sem)
    s8[...] = fac.reshape(1024, 128)[...].astype(F32)
    halves = [s8[pl.ds(q, 128, stride=8), :] for q in range(8)]
    lefts = [
        jnp.concatenate(
            [halves[2 * r + kh] * mask_v[kh : kh + 1, :] for kh in range(2)], axis=1
        )
        for r in range(2)
    ]
    left = jnp.concatenate(lefts, axis=0).astype(BF16)
    rights = [jnp.concatenate(halves[4 + 2 * r : 6 + 2 * r], axis=1) for r in range(2)]
    right = jnp.concatenate(rights, axis=0).astype(BF16)
    product = lax.dot_general(right, left, NT, preferred_element_type=F32)
    for rj, ri in itertools.product(range(2), range(2)):
        s4[pl.ds(2 * rj + ri, 128, stride=4), :] = product[
            128 * rj : 128 * rj + 128, 128 * ri : 128 * ri + 128
        ]
    prod.reshape(512, 128)[...] = s4[...].astype(BF16)
    for t in targets:
        send(prod.at[t], prods.at[me], send_sem.at[2], prods_sem, t)
    pltpu.make_async_copy(prod.at[me], prods.at[me], prods_sem).start()

    landed(pairs, pairs_sem)
    columns = pairs.reshape(512, 128)
    normed = layer_norm(columns[...].astype(F32), 1).astype(BF16)
    gate_v[...] = jax.nn.sigmoid(
        jnp.dot(normed, w_v[4], preferred_element_type=F32)
    )

    landed(prods, prods_sem)
    s4[...] = prods.reshape(512, 128)[...].astype(F32)
    update = []
    for rj, ri in itertools.product(range(2), range(2)):
        channels = s4[pl.ds(2 * rj + ri, 128, stride=4), :]
        update.append(
            lax.dot_general(
                layer_norm(channels, 0).astype(BF16), w_v[5], TN, preferred_element_type=F32
            )
        )
    for (rj, ri), part in zip(itertools.product(range(2), range(2)), update):
        s4[pl.ds(2 * ri + rj, 128, stride=4), :] = part
    out_ref[...] = (columns[...].astype(F32) + gate_v[...] * s4[...]).astype(BF16)

    landed(msg.at[pl.ds(0, D - 1)], send_sem.at[0])
    landed(pairs.at[pl.ds(0, D - 1)], send_sem.at[1])
    landed(prod.at[pl.ds(0, D - 1)], send_sem.at[2])
    landed(mx.at[pl.ds(0, 7)], mask_sem.at[0])
    landed(my.at[pl.ds(0, 15)], mask_sem.at[2])


def body(pair, residue_mask, *weights):
    hbm = pl.BlockSpec(memory_space=pltpu.HBM)
    inputs = [
        pltpu.with_memory_space_constraint(v, pltpu.HBM)
        for v in (pair.reshape(2, D, 2, 128), *weights)
    ]
    out = pl.pallas_call(
        kernel,
        out_shape=pltpu.VMEM((512, 128), BF16),
        in_specs=[hbm, pl.BlockSpec(memory_space=pltpu.SMEM)] + [hbm] * 6,
        out_specs=pl.BlockSpec(memory_space=pltpu.VMEM),
        scratch_shapes=[
            pltpu.VMEM((2, D, 2, 128), BF16),
            pltpu.VMEM((6, 128, 128), BF16),
            pltpu.VMEM((D, 8, 128), BF16),
            pltpu.VMEM((D, 8, 128), BF16),
            pltpu.VMEM((D, 4, 128), BF16),
            pltpu.VMEM((D, 4, 128), BF16),
            pltpu.VMEM((D, 2, 2, 128), BF16),
            pltpu.VMEM((8, 2, 128), F32),
            pltpu.VMEM((16, 2, 128), F32),
            pltpu.VMEM((2, 128), F32),
            pltpu.VMEM((1024, 128), F32),
            pltpu.VMEM((512, 128), F32),
            pltpu.VMEM((512, 128), F32),
            pltpu.SemaphoreType.DMA,
            pltpu.SemaphoreType.DMA((6,)),
            pltpu.SemaphoreType.DMA((3,)),
            pltpu.SemaphoreType.DMA,
            pltpu.SemaphoreType.DMA,
            pltpu.SemaphoreType.DMA,
            pltpu.SemaphoreType.DMA((4,)),
        ],
        compiler_params=pltpu.CompilerParams(
            collective_id=0, has_side_effects=True, vmem_limit_bytes=60 << 20
        ),
    )(inputs[0], residue_mask, *inputs[1:])
    return out.reshape(256, 2, 128)


def solution(mesh):
    return jax.shard_map(
        body,
        mesh=mesh,
        in_specs=(P(("batch", "axial"), None, None), P(("batch", "axial")))
        + (P(),) * 6,
        out_specs=P("batch", "axial", None),
        check_vma=False,
    )
```

```python
import itertools

import jax
import jax.numpy as jnp
from jax import lax
from jax.experimental import pallas as pl
from jax.experimental.pallas import tpu as pltpu
from jax.sharding import PartitionSpec as P

MESH = pl.DeviceIdType.MESH
F32, BF16 = jnp.float32, jnp.bfloat16
NZ, NY, NX, NC = 2, 8, 4, 2
D = NZ * NY * NX * NC
CH = 128
Y_ORDER = (4, 3, 5, 2, 6, 1, 7, 0)
X_ORDER = (2, 1, 3, 0)
PEERS = tuple(
    (dz, dy, dx, dc)
    for dy, dx, dz, dc in itertools.product(Y_ORDER, X_ORDER, (1, 0), (0, 1))
    if dz + dy + dx + dc
)
EARLY = 112
NT = (((1,), (1,)), ((), ()))
TN = (((0,), (0,)), ((), ()))


def layer_norm(values, axis):
    mean = jnp.mean(values, axis=axis, keepdims=True)
    centered = values - mean
    var = jnp.mean(centered * centered, axis=axis, keepdims=True)
    return centered * lax.rsqrt(var + 1e-05)


def kernel(
    pair_hbm, mask_hbm, gl_hbm, pl_hbm, gr_hbm, pr_hbm, go_hbm, po_hbm, out_ref,
    mask_ref, pair_v, w_v, msg, fac, prod, prods, pairs, mx, my, mask_v, s8, s4, gate_v,
    load_sem, mask_load_sem, wload_sem, send_sem, fac_sem, prods_sem, pairs_sem, mask_sem,
):
    me = lax.axis_index("axial")
    z, y = lax.div(me, 64), lax.rem(lax.div(me, 8), 8)
    x, c = lax.rem(lax.div(me, 2), 4), lax.rem(me, 2)
    zt = [64 * lax.rem(z + k, 2) for k in range(NZ)]
    yt = [8 * lax.rem(y + k, 8) for k in range(NY)]
    xt = [2 * lax.rem(x + k, 4) for k in range(NX)]
    ct = [lax.rem(c + k, 2) for k in range(NC)]
    targets = [zt[dz] + yt[dy] + xt[dx] + ct[dc] for dz, dy, dx, dc in PEERS]

    barrier = pltpu.get_barrier_semaphore()
    for t in targets:
        pl.semaphore_signal(barrier, inc=1, device_id={"axial": t}, device_id_type=MESH)

    load = pltpu.make_async_copy(pair_hbm, pair_v, load_sem)
    load.start()
    mask_load = pltpu.make_async_copy(mask_hbm, mask_ref, mask_load_sem)
    mask_load.start()
    wloads = [
        pltpu.make_async_copy(ref, w_v.at[i], wload_sem.at[i])
        for i, ref in enumerate((gl_hbm, pl_hbm, gr_hbm, pr_hbm, go_hbm, po_hbm))
    ]
    for w in wloads:
        w.start()

    def send(src, dst, sem, recv_sem, t):
        pltpu.make_async_remote_copy(
            src_ref=src, dst_ref=dst, send_sem=sem, recv_sem=recv_sem,
            device_id={"axial": t}, device_id_type=MESH,
        ).start()

    def landed(ref, sem):
        pltpu.make_async_copy(ref, ref, sem).wait()

    load.wait()
    normed = layer_norm(pair_v.reshape(512, 128)[...].astype(F32), 1).astype(BF16)
    for w in wloads:
        w.wait()
    mask_load.wait()
    for f in range(2):
        gating = lax.dot_general(
            w_v[2 * f], normed, (((0,), (1,)), ((), ())), preferred_element_type=F32
        )
        values = lax.dot_general(
            w_v[2 * f + 1], normed, (((0,), (1,)), ((), ())), preferred_element_type=F32
        )
        factor = jax.nn.sigmoid(gating) * values
        for r in range(2):
            row_mask = mask_ref[r].astype(F32)
            for kh in range(2):
                q = 2 * r + kh
                s8[pl.ds(4 * f + q, 128, stride=8), :] = (
                    factor[:, 128 * q : 128 * q + 128] * row_mask
                )
    msg.reshape(1024, 128)[...] = s8[...].astype(BF16)

    k_index = lax.broadcasted_iota(jnp.int32, (2, 128), 0) * 128 + lax.broadcasted_iota(
        jnp.int32, (2, 128), 1
    )
    own_mask = jnp.where(k_index == 2 * me, mask_ref[0], 0) + jnp.where(
        k_index == 2 * me + 1, mask_ref[1], 0
    )
    xc, zy = 2 * x + c, 8 * z + y
    mx[xc] = own_mask.astype(F32)

    pl.semaphore_wait(barrier, D - 1)

    for dx, dc in itertools.product(range(NX), range(NC)):
        if dx + dc:
            t = zt[0] + yt[0] + xt[dx] + ct[dc]
            send(mx.at[xc], mx.at[xc], mask_sem.at[0], mask_sem.at[1], t)
    for t in targets[:EARLY]:
        send(msg.at[t], fac.at[me], send_sem.at[0], fac_sem, t)
    landed(mx.at[pl.ds(0, 7)], mask_sem.at[1])
    my[zy] = jnp.sum(mx[...], axis=0)
    for dy, dz in itertools.product(Y_ORDER, (1, 0)):
        if dy + dz:
            t = zt[dz] + yt[dy] + xt[0] + ct[0]
            send(my.at[zy], my.at[zy], mask_sem.at[2], mask_sem.at[3], t)
    for t in targets[EARLY:]:
        send(msg.at[t], fac.at[me], send_sem.at[0], fac_sem, t)
    pltpu.make_async_copy(msg.at[me], fac.at[me], fac_sem).start()
    for t in targets:
        send(pair_v.at[:, t], pairs.at[me], send_sem.at[1], pairs_sem, t)
    pltpu.make_async_copy(pair_v.at[:, me], pairs.at[me], pairs_sem).start()
    landed(my.at[pl.ds(0, 15)], mask_sem.at[3])
    mask_v[...] = jnp.sum(my[...], axis=0)

    landed(fac, fac_sem)
    s8[...] = fac.reshape(1024, 128)[...].astype(F32)
    halves = [s8[pl.ds(q, 128, stride=8), :] for q in range(8)]
    lefts = [
        jnp.concatenate(
            [halves[2 * r + kh] * mask_v[kh : kh + 1, :] for kh in range(2)], axis=1
        )
        for r in range(2)
    ]
    left = jnp.concatenate(lefts, axis=0).astype(BF16)
    rights = [jnp.concatenate(halves[4 + 2 * r : 6 + 2 * r], axis=1) for r in range(2)]
    right = jnp.concatenate(rights, axis=0).astype(BF16)
    product = lax.dot_general(right, left, NT, preferred_element_type=F32)
    for rj, ri in itertools.product(range(2), range(2)):
        s4[pl.ds(2 * rj + ri, 128, stride=4), :] = product[
            128 * rj : 128 * rj + 128, 128 * ri : 128 * ri + 128
        ]
    prod.reshape(512, 128)[...] = s4[...].astype(BF16)
    for pz, py in [(0, 0), (0, 1), (0, 2), (0, 3), (1, 0), (0, 7), (1, 1), (0, 6), (0, 5), (0, 4), (1, 2), (1, 3), (1, 7), (1, 6), (1, 5), (1, 4)]:
        for dx, dc in itertools.product(X_ORDER, (1, 0)):
            t = 64 * pz + 8 * py + xt[dx] + ct[dc]

            def send_prod(t=t):
                send(prod.at[t], prods.at[me], send_sem.at[2], prods_sem, t)

            if dx + dc:
                send_prod()
            else:
                pl.when(t != me)(send_prod)
    pltpu.make_async_copy(prod.at[me], prods.at[me], prods_sem).start()

    landed(pairs, pairs_sem)
    columns = pairs.reshape(512, 128)
    normed = layer_norm(columns[...].astype(F32), 1).astype(BF16)
    gate_v[...] = jax.nn.sigmoid(
        jnp.dot(normed, w_v[4], preferred_element_type=F32)
    )

    landed(prods, prods_sem)
    s4[...] = prods.reshape(512, 128)[...].astype(F32)
    update = []
    for rj, ri in itertools.product(range(2), range(2)):
        channels = s4[pl.ds(2 * rj + ri, 128, stride=4), :]
        update.append(
            lax.dot_general(
                layer_norm(channels, 0).astype(BF16), w_v[5], TN, preferred_element_type=F32
            )
        )
    for (rj, ri), part in zip(itertools.product(range(2), range(2)), update):
        s4[pl.ds(2 * ri + rj, 128, stride=4), :] = part
    out_ref[...] = (columns[...].astype(F32) + gate_v[...] * s4[...]).astype(BF16)

    landed(msg.at[pl.ds(0, D - 1)], send_sem.at[0])
    landed(pairs.at[pl.ds(0, D - 1)], send_sem.at[1])
    landed(prod.at[pl.ds(0, D - 1)], send_sem.at[2])
    landed(mx.at[pl.ds(0, 7)], mask_sem.at[0])
    landed(my.at[pl.ds(0, 15)], mask_sem.at[2])


def body(pair, residue_mask, *weights):
    hbm = pl.BlockSpec(memory_space=pltpu.HBM)
    inputs = [
        pltpu.with_memory_space_constraint(v, pltpu.HBM)
        for v in (pair.reshape(2, D, 2, 128), residue_mask, *weights)
    ]
    out = pl.pallas_call(
        kernel,
        out_shape=pltpu.VMEM((512, 128), BF16),
        in_specs=[hbm] * 8,
        out_specs=pl.BlockSpec(memory_space=pltpu.VMEM),
        scratch_shapes=[
            pltpu.SMEM((2,), jnp.int32),
            pltpu.VMEM((2, D, 2, 128), BF16),
            pltpu.VMEM((6, 128, 128), BF16),
            pltpu.VMEM((D, 8, 128), BF16),
            pltpu.VMEM((D, 8, 128), BF16),
            pltpu.VMEM((D, 4, 128), BF16),
            pltpu.VMEM((D, 4, 128), BF16),
            pltpu.VMEM((D, 2, 2, 128), BF16),
            pltpu.VMEM((8, 2, 128), F32),
            pltpu.VMEM((16, 2, 128), F32),
            pltpu.VMEM((2, 128), F32),
            pltpu.VMEM((1024, 128), F32),
            pltpu.VMEM((512, 128), F32),
            pltpu.VMEM((512, 128), F32),
            pltpu.SemaphoreType.DMA,
            pltpu.SemaphoreType.DMA,
            pltpu.SemaphoreType.DMA((6,)),
            pltpu.SemaphoreType.DMA((3,)),
            pltpu.SemaphoreType.DMA,
            pltpu.SemaphoreType.DMA,
            pltpu.SemaphoreType.DMA,
            pltpu.SemaphoreType.DMA((4,)),
        ],
        compiler_params=pltpu.CompilerParams(
            collective_id=0, has_side_effects=True, vmem_limit_bytes=60 << 20
        ),
    )(*inputs)
    return out.reshape(256, 2, 128)


def solution(mesh):
    return jax.shard_map(
        body,
        mesh=mesh,
        in_specs=(P(("batch", "axial"), None, None), P(("batch", "axial")))
        + (P(),) * 6,
        out_specs=P("batch", "axial", None),
        check_vma=False,
    )
```

```python
import itertools

import jax
import jax.numpy as jnp
from jax import lax
from jax.experimental import pallas as pl
from jax.experimental.pallas import tpu as pltpu
from jax.sharding import PartitionSpec as P

MESH = pl.DeviceIdType.MESH
F32, BF16 = jnp.float32, jnp.bfloat16
NZ, NY, NX, NC = 2, 8, 4, 2
D = NZ * NY * NX * NC
CH = 128
Y_ORDER = (4, 3, 5, 2, 6, 1, 7, 0)
X_ORDER = (2, 1, 3, 0)
PEERS = tuple(
    (dz, dy, dx, dc)
    for dy, dx, dz, dc in itertools.product(Y_ORDER, X_ORDER, (1, 0), (0, 1))
    if dz + dy + dx + dc
)
EARLY = 60
NT = (((1,), (1,)), ((), ()))
TN = (((0,), (0,)), ((), ()))


def layer_norm(values, axis):
    mean = jnp.mean(values, axis=axis, keepdims=True)
    centered = values - mean
    var = jnp.mean(centered * centered, axis=axis, keepdims=True)
    return centered * lax.rsqrt(var + 1e-05)


def kernel(
    pair_hbm, mask_hbm, gl_hbm, pl_hbm, gr_hbm, pr_hbm, go_hbm, po_hbm, out_ref,
    mask_ref, pair_v, w_v, msg, fac, prod, prods, pairs, mx, my, mask_v, s8, s4, gate_v,
    load_sem, mask_load_sem, wload_sem, send_sem, fac_sem, prods_sem, pairs_sem, mask_sem,
):
    me = lax.axis_index("axial")
    z, y = lax.div(me, 64), lax.rem(lax.div(me, 8), 8)
    x, c = lax.rem(lax.div(me, 2), 4), lax.rem(me, 2)
    zt = [64 * lax.rem(z + k, 2) for k in range(NZ)]
    yt = [8 * lax.rem(y + k, 8) for k in range(NY)]
    xt = [2 * lax.rem(x + k, 4) for k in range(NX)]
    ct = [lax.rem(c + k, 2) for k in range(NC)]
    targets = [zt[dz] + yt[dy] + xt[dx] + ct[dc] for dz, dy, dx, dc in PEERS]

    barrier = pltpu.get_barrier_semaphore()
    for t in targets:
        pl.semaphore_signal(barrier, inc=1, device_id={"axial": t}, device_id_type=MESH)

    load = pltpu.make_async_copy(pair_hbm, pair_v, load_sem)
    load.start()
    mask_load = pltpu.make_async_copy(mask_hbm, mask_ref, mask_load_sem)
    mask_load.start()
    wloads = [
        pltpu.make_async_copy(ref, w_v.at[i], wload_sem.at[i])
        for i, ref in enumerate((gl_hbm, pl_hbm, gr_hbm, pr_hbm, go_hbm, po_hbm))
    ]
    for w in wloads:
        w.start()

    def send(src, dst, sem, recv_sem, t):
        pltpu.make_async_remote_copy(
            src_ref=src, dst_ref=dst, send_sem=sem, recv_sem=recv_sem,
            device_id={"axial": t}, device_id_type=MESH,
        ).start()

    def landed(ref, sem):
        pltpu.make_async_copy(ref, ref, sem).wait()

    load.wait()
    normed = layer_norm(pair_v.reshape(512, 128)[...].astype(F32), 1).astype(BF16)
    for w in wloads:
        w.wait()
    mask_load.wait()
    for f in range(2):
        gating = lax.dot_general(
            w_v[2 * f], normed, (((0,), (1,)), ((), ())), preferred_element_type=F32
        )
        values = lax.dot_general(
            w_v[2 * f + 1], normed, (((0,), (1,)), ((), ())), preferred_element_type=F32
        )
        factor = jax.nn.sigmoid(gating) * values
        for r in range(2):
            row_mask = mask_ref[r].astype(F32)
            for kh in range(2):
                q = 2 * r + kh
                s8[pl.ds(4 * f + q, 128, stride=8), :] = (
                    factor[:, 128 * q : 128 * q + 128] * row_mask
                )
    msg.reshape(1024, 128)[...] = s8[...].astype(BF16)

    k_index = lax.broadcasted_iota(jnp.int32, (2, 128), 0) * 128 + lax.broadcasted_iota(
        jnp.int32, (2, 128), 1
    )
    own_mask = jnp.where(k_index == 2 * me, mask_ref[0], 0) + jnp.where(
        k_index == 2 * me + 1, mask_ref[1], 0
    )
    xc, zy = 2 * x + c, 8 * z + y
    mx[xc] = own_mask.astype(F32)

    pl.semaphore_wait(barrier, D - 1)

    for dx, dc in itertools.product(range(NX), range(NC)):
        if dx + dc:
            t = zt[0] + yt[0] + xt[dx] + ct[dc]
            send(mx.at[xc], mx.at[xc], mask_sem.at[0], mask_sem.at[1], t)
    for t in targets[:EARLY]:
        send(msg.at[t], fac.at[me], send_sem.at[0], fac_sem, t)
    landed(mx.at[pl.ds(0, 7)], mask_sem.at[1])
    my[zy] = jnp.sum(mx[...], axis=0)
    for dy, dz in itertools.product(Y_ORDER, (1, 0)):
        if dy + dz:
            t = zt[dz] + yt[dy] + xt[0] + ct[0]
            send(my.at[zy], my.at[zy], mask_sem.at[2], mask_sem.at[3], t)
    for t in targets[EARLY:]:
        send(msg.at[t], fac.at[me], send_sem.at[0], fac_sem, t)
    pltpu.make_async_copy(msg.at[me], fac.at[me], fac_sem).start()
    for t in targets:
        send(pair_v.at[:, t], pairs.at[me], send_sem.at[1], pairs_sem, t)
    pltpu.make_async_copy(pair_v.at[:, me], pairs.at[me], pairs_sem).start()
    landed(my.at[pl.ds(0, 15)], mask_sem.at[3])
    mask_v[...] = jnp.sum(my[...], axis=0)

    landed(fac, fac_sem)
    s8[...] = fac.reshape(1024, 128)[...].astype(F32)
    halves = [s8[pl.ds(q, 128, stride=8), :] for q in range(8)]
    lefts = [
        jnp.concatenate(
            [halves[2 * r + kh] * mask_v[kh : kh + 1, :] for kh in range(2)], axis=1
        )
        for r in range(2)
    ]
    left = jnp.concatenate(lefts, axis=0).astype(BF16)
    rights = [jnp.concatenate(halves[4 + 2 * r : 6 + 2 * r], axis=1) for r in range(2)]
    right = jnp.concatenate(rights, axis=0).astype(BF16)
    product = lax.dot_general(right, left, NT, preferred_element_type=F32)
    for rj, ri in itertools.product(range(2), range(2)):
        s4[pl.ds(2 * rj + ri, 128, stride=4), :] = product[
            128 * rj : 128 * rj + 128, 128 * ri : 128 * ri + 128
        ]
    prod.reshape(512, 128)[...] = s4[...].astype(BF16)
    for pz, py in [(0, 0), (0, 1), (0, 2), (0, 3), (1, 0), (0, 7), (1, 1), (0, 6), (0, 5), (0, 4), (1, 2), (1, 3), (1, 7), (1, 6), (1, 5), (1, 4)]:
        for dx, dc in itertools.product(X_ORDER, (1, 0)):
            t = 64 * pz + 8 * py + xt[dx] + ct[dc]

            def send_prod(t=t):
                send(prod.at[t], prods.at[me], send_sem.at[2], prods_sem, t)

            if dx + dc:
                send_prod()
            else:
                pl.when(t != me)(send_prod)
    pltpu.make_async_copy(prod.at[me], prods.at[me], prods_sem).start()

    landed(pairs, pairs_sem)
    columns = pairs.reshape(512, 128)
    normed = layer_norm(columns[...].astype(F32), 1).astype(BF16)
    gate_v[...] = jax.nn.sigmoid(
        jnp.dot(normed, w_v[4], preferred_element_type=F32)
    )

    landed(prods, prods_sem)
    s4[...] = prods.reshape(512, 128)[...].astype(F32)
    update = []
    for rj, ri in itertools.product(range(2), range(2)):
        channels = s4[pl.ds(2 * rj + ri, 128, stride=4), :]
        update.append(
            lax.dot_general(
                layer_norm(channels, 0).astype(BF16), w_v[5], TN, preferred_element_type=F32
            )
        )
    for (rj, ri), part in zip(itertools.product(range(2), range(2)), update):
        s4[pl.ds(2 * ri + rj, 128, stride=4), :] = part
    out_ref[...] = (columns[...].astype(F32) + gate_v[...] * s4[...]).astype(BF16)

    landed(msg.at[pl.ds(0, D - 1)], send_sem.at[0])
    landed(pairs.at[pl.ds(0, D - 1)], send_sem.at[1])
    landed(prod.at[pl.ds(0, D - 1)], send_sem.at[2])
    landed(mx.at[pl.ds(0, 7)], mask_sem.at[0])
    landed(my.at[pl.ds(0, 15)], mask_sem.at[2])


def body(pair, residue_mask, *weights):
    hbm = pl.BlockSpec(memory_space=pltpu.HBM)
    inputs = [
        pltpu.with_memory_space_constraint(v, pltpu.HBM)
        for v in (pair.reshape(2, D, 2, 128), residue_mask, *weights)
    ]
    out = pl.pallas_call(
        kernel,
        out_shape=pltpu.VMEM((512, 128), BF16),
        in_specs=[hbm] * 8,
        out_specs=pl.BlockSpec(memory_space=pltpu.VMEM),
        scratch_shapes=[
            pltpu.SMEM((2,), jnp.int32),
            pltpu.VMEM((2, D, 2, 128), BF16),
            pltpu.VMEM((6, 128, 128), BF16),
            pltpu.VMEM((D, 8, 128), BF16),
            pltpu.VMEM((D, 8, 128), BF16),
            pltpu.VMEM((D, 4, 128), BF16),
            pltpu.VMEM((D, 4, 128), BF16),
            pltpu.VMEM((D, 2, 2, 128), BF16),
            pltpu.VMEM((8, 2, 128), F32),
            pltpu.VMEM((16, 2, 128), F32),
            pltpu.VMEM((2, 128), F32),
            pltpu.VMEM((1024, 128), F32),
            pltpu.VMEM((512, 128), F32),
            pltpu.VMEM((512, 128), F32),
            pltpu.SemaphoreType.DMA,
            pltpu.SemaphoreType.DMA,
            pltpu.SemaphoreType.DMA((6,)),
            pltpu.SemaphoreType.DMA((3,)),
            pltpu.SemaphoreType.DMA,
            pltpu.SemaphoreType.DMA,
            pltpu.SemaphoreType.DMA,
            pltpu.SemaphoreType.DMA((4,)),
        ],
        compiler_params=pltpu.CompilerParams(
            collective_id=0, has_side_effects=True, vmem_limit_bytes=60 << 20
        ),
    )(*inputs)
    return out.reshape(256, 2, 128)


def solution(mesh):
    return jax.shard_map(
        body,
        mesh=mesh,
        in_specs=(P(("batch", "axial"), None, None), P(("batch", "axial")))
        + (P(),) * 6,
        out_specs=P("batch", "axial", None),
        check_vma=False,
    )
```

```python
import itertools

import jax
import jax.numpy as jnp
from jax import lax
from jax.experimental import pallas as pl
from jax.experimental.pallas import tpu as pltpu
from jax.sharding import PartitionSpec as P

MESH = pl.DeviceIdType.MESH
F32, BF16 = jnp.float32, jnp.bfloat16
NZ, NY, NX, NC = 2, 8, 4, 2
D = NZ * NY * NX * NC
CH = 128
Y_ORDER = (4, 3, 5, 2, 6, 1, 7, 0)
X_ORDER = (2, 1, 3, 0)
PEERS = tuple(
    sorted(
        (d for d in itertools.product(range(NZ), range(NY), range(NX), range(NC)) if any(d)),
        key=lambda d: (
            -(d[0] + min(d[1], NY - d[1]) + min(d[2], NX - d[2])),
            -min(d[1], NY - d[1]),
            d[2],
            d[3],
            d[1],
        ),
    )
)
EARLY = 60
NT = (((1,), (1,)), ((), ()))
TN = (((0,), (0,)), ((), ()))


def layer_norm(values, axis):
    mean = jnp.mean(values, axis=axis, keepdims=True)
    centered = values - mean
    var = jnp.mean(centered * centered, axis=axis, keepdims=True)
    return centered * lax.rsqrt(var + 1e-05)


def kernel(
    pair_hbm, mask_hbm, gl_hbm, pl_hbm, gr_hbm, pr_hbm, go_hbm, po_hbm, out_ref,
    mask_ref, pair_v, w_v, msg, fac, prod, prods, pairs, mx, my, mask_v, s8, s4, gate_v,
    load_sem, mask_load_sem, wload_sem, send_sem, fac_sem, prods_sem, pairs_sem, mask_sem,
):
    me = lax.axis_index("axial")
    z, y = lax.div(me, 64), lax.rem(lax.div(me, 8), 8)
    x, c = lax.rem(lax.div(me, 2), 4), lax.rem(me, 2)
    zt = [64 * lax.rem(z + k, 2) for k in range(NZ)]
    yt = [8 * lax.rem(y + k, 8) for k in range(NY)]
    xt = [2 * lax.rem(x + k, 4) for k in range(NX)]
    ct = [lax.rem(c + k, 2) for k in range(NC)]
    targets = [zt[dz] + yt[dy] + xt[dx] + ct[dc] for dz, dy, dx, dc in PEERS]

    barrier = pltpu.get_barrier_semaphore()
    for t in targets:
        pl.semaphore_signal(barrier, inc=1, device_id={"axial": t}, device_id_type=MESH)

    load = pltpu.make_async_copy(pair_hbm, pair_v, load_sem)
    load.start()
    mask_load = pltpu.make_async_copy(mask_hbm, mask_ref, mask_load_sem)
    mask_load.start()
    wloads = [
        pltpu.make_async_copy(ref, w_v.at[i], wload_sem.at[i])
        for i, ref in enumerate((gl_hbm, pl_hbm, gr_hbm, pr_hbm, go_hbm, po_hbm))
    ]
    for w in wloads:
        w.start()

    def send(src, dst, sem, recv_sem, t):
        pltpu.make_async_remote_copy(
            src_ref=src, dst_ref=dst, send_sem=sem, recv_sem=recv_sem,
            device_id={"axial": t}, device_id_type=MESH,
        ).start()

    def landed(ref, sem):
        pltpu.make_async_copy(ref, ref, sem).wait()

    load.wait()
    normed = layer_norm(pair_v.reshape(512, 128)[...].astype(F32), 1).astype(BF16)
    for w in wloads:
        w.wait()
    mask_load.wait()
    for f in range(2):
        gating = lax.dot_general(
            w_v[2 * f], normed, (((0,), (1,)), ((), ())), preferred_element_type=F32
        )
        values = lax.dot_general(
            w_v[2 * f + 1], normed, (((0,), (1,)), ((), ())), preferred_element_type=F32
        )
        factor = jax.nn.sigmoid(gating) * values
        for r in range(2):
            row_mask = mask_ref[r].astype(F32)
            for kh in range(2):
                q = 2 * r + kh
                s8[pl.ds(4 * f + q, 128, stride=8), :] = (
                    factor[:, 128 * q : 128 * q + 128] * row_mask
                )
    msg.reshape(1024, 128)[...] = s8[...].astype(BF16)

    k_index = lax.broadcasted_iota(jnp.int32, (2, 128), 0) * 128 + lax.broadcasted_iota(
        jnp.int32, (2, 128), 1
    )
    own_mask = jnp.where(k_index == 2 * me, mask_ref[0], 0) + jnp.where(
        k_index == 2 * me + 1, mask_ref[1], 0
    )
    xc, zy = 2 * x + c, 8 * z + y
    mx[xc] = own_mask.astype(F32)

    pl.semaphore_wait(barrier, D - 1)

    for dx, dc in itertools.product(range(NX), range(NC)):
        if dx + dc:
            t = zt[0] + yt[0] + xt[dx] + ct[dc]
            send(mx.at[xc], mx.at[xc], mask_sem.at[0], mask_sem.at[1], t)
    for t in targets[:EARLY]:
        send(msg.at[t], fac.at[me], send_sem.at[0], fac_sem, t)
    landed(mx.at[pl.ds(0, 7)], mask_sem.at[1])
    my[zy] = jnp.sum(mx[...], axis=0)
    for dy, dz in itertools.product(Y_ORDER, (1, 0)):
        if dy + dz:
            t = zt[dz] + yt[dy] + xt[0] + ct[0]
            send(my.at[zy], my.at[zy], mask_sem.at[2], mask_sem.at[3], t)
    for t in targets[EARLY:]:
        send(msg.at[t], fac.at[me], send_sem.at[0], fac_sem, t)
    pltpu.make_async_copy(msg.at[me], fac.at[me], fac_sem).start()
    for t in targets:
        send(pair_v.at[:, t], pairs.at[me], send_sem.at[1], pairs_sem, t)
    pltpu.make_async_copy(pair_v.at[:, me], pairs.at[me], pairs_sem).start()
    landed(my.at[pl.ds(0, 15)], mask_sem.at[3])
    mask_v[...] = jnp.sum(my[...], axis=0)

    landed(fac, fac_sem)
    s8[...] = fac.reshape(1024, 128)[...].astype(F32)
    halves = [s8[pl.ds(q, 128, stride=8), :] for q in range(8)]
    lefts = [
        jnp.concatenate(
            [halves[2 * r + kh] * mask_v[kh : kh + 1, :] for kh in range(2)], axis=1
        )
        for r in range(2)
    ]
    left = jnp.concatenate(lefts, axis=0).astype(BF16)
    rights = [jnp.concatenate(halves[4 + 2 * r : 6 + 2 * r], axis=1) for r in range(2)]
    right = jnp.concatenate(rights, axis=0).astype(BF16)
    product = lax.dot_general(right, left, NT, preferred_element_type=F32)
    for rj, ri in itertools.product(range(2), range(2)):
        s4[pl.ds(2 * rj + ri, 128, stride=4), :] = product[
            128 * rj : 128 * rj + 128, 128 * ri : 128 * ri + 128
        ]
    prod.reshape(512, 128)[...] = s4[...].astype(BF16)
    for pz, py in [(0, 0), (0, 1), (0, 2), (0, 3), (1, 0), (0, 7), (1, 1), (0, 6), (0, 5), (0, 4), (1, 2), (1, 3), (1, 7), (1, 6), (1, 5), (1, 4)]:
        for dx, dc in itertools.product(X_ORDER, (1, 0)):
            t = 64 * pz + 8 * py + xt[dx] + ct[dc]

            def send_prod(t=t):
                send(prod.at[t], prods.at[me], send_sem.at[2], prods_sem, t)

            if dx + dc:
                send_prod()
            else:
                pl.when(t != me)(send_prod)
    pltpu.make_async_copy(prod.at[me], prods.at[me], prods_sem).start()

    landed(pairs, pairs_sem)
    columns = pairs.reshape(512, 128)
    normed = layer_norm(columns[...].astype(F32), 1).astype(BF16)
    gate_v[...] = jax.nn.sigmoid(
        jnp.dot(normed, w_v[4], preferred_element_type=F32)
    )

    landed(prods, prods_sem)
    s4[...] = prods.reshape(512, 128)[...].astype(F32)
    update = []
    for rj, ri in itertools.product(range(2), range(2)):
        channels = s4[pl.ds(2 * rj + ri, 128, stride=4), :]
        update.append(
            lax.dot_general(
                layer_norm(channels, 0).astype(BF16), w_v[5], TN, preferred_element_type=F32
            )
        )
    for (rj, ri), part in zip(itertools.product(range(2), range(2)), update):
        s4[pl.ds(2 * ri + rj, 128, stride=4), :] = part
    out_ref[...] = (columns[...].astype(F32) + gate_v[...] * s4[...]).astype(BF16)

    landed(msg.at[pl.ds(0, D - 1)], send_sem.at[0])
    landed(pairs.at[pl.ds(0, D - 1)], send_sem.at[1])
    landed(prod.at[pl.ds(0, D - 1)], send_sem.at[2])
    landed(mx.at[pl.ds(0, 7)], mask_sem.at[0])
    landed(my.at[pl.ds(0, 15)], mask_sem.at[2])


def body(pair, residue_mask, *weights):
    hbm = pl.BlockSpec(memory_space=pltpu.HBM)
    inputs = [
        pltpu.with_memory_space_constraint(v, pltpu.HBM)
        for v in (pair.reshape(2, D, 2, 128), residue_mask, *weights)
    ]
    out = pl.pallas_call(
        kernel,
        out_shape=pltpu.VMEM((512, 128), BF16),
        in_specs=[hbm] * 8,
        out_specs=pl.BlockSpec(memory_space=pltpu.VMEM),
        scratch_shapes=[
            pltpu.SMEM((2,), jnp.int32),
            pltpu.VMEM((2, D, 2, 128), BF16),
            pltpu.VMEM((6, 128, 128), BF16),
            pltpu.VMEM((D, 8, 128), BF16),
            pltpu.VMEM((D, 8, 128), BF16),
            pltpu.VMEM((D, 4, 128), BF16),
            pltpu.VMEM((D, 4, 128), BF16),
            pltpu.VMEM((D, 2, 2, 128), BF16),
            pltpu.VMEM((8, 2, 128), F32),
            pltpu.VMEM((16, 2, 128), F32),
            pltpu.VMEM((2, 128), F32),
            pltpu.VMEM((1024, 128), F32),
            pltpu.VMEM((512, 128), F32),
            pltpu.VMEM((512, 128), F32),
            pltpu.SemaphoreType.DMA,
            pltpu.SemaphoreType.DMA,
            pltpu.SemaphoreType.DMA((6,)),
            pltpu.SemaphoreType.DMA((3,)),
            pltpu.SemaphoreType.DMA,
            pltpu.SemaphoreType.DMA,
            pltpu.SemaphoreType.DMA,
            pltpu.SemaphoreType.DMA((4,)),
        ],
        compiler_params=pltpu.CompilerParams(
            collective_id=0, has_side_effects=True, vmem_limit_bytes=60 << 20
        ),
    )(*inputs)
    return out.reshape(256, 2, 128)


def solution(mesh):
    return jax.shard_map(
        body,
        mesh=mesh,
        in_specs=(P(("batch", "axial"), None, None), P(("batch", "axial")))
        + (P(),) * 6,
        out_specs=P("batch", "axial", None),
        check_vma=False,
    )
```

```python
import itertools

import jax
import jax.numpy as jnp
from jax import lax
from jax.experimental import pallas as pl
from jax.experimental.pallas import tpu as pltpu
from jax.sharding import PartitionSpec as P

MESH = pl.DeviceIdType.MESH
F32, BF16 = jnp.float32, jnp.bfloat16
NZ, NY, NX, NC = 2, 8, 4, 2
D = NZ * NY * NX * NC
CH = 128
Y_ORDER = (4, 3, 5, 2, 6, 1, 7, 0)
X_ORDER = (2, 1, 3, 0)
PEERS = tuple(
    sorted(
        (d for d in itertools.product(range(NZ), range(NY), range(NX), range(NC)) if any(d)),
        key=lambda d: (
            -(d[0] + min(d[1], NY - d[1]) + min(d[2], NX - d[2])),
            -min(d[1], NY - d[1]),
            d[2],
            d[3],
            d[1],
        ),
    )
)
EARLY = 60
NT = (((1,), (1,)), ((), ()))
TN = (((0,), (0,)), ((), ()))


def layer_norm(values, axis):
    mean = jnp.mean(values, axis=axis, keepdims=True)
    centered = values - mean
    var = jnp.mean(centered * centered, axis=axis, keepdims=True)
    return centered * lax.rsqrt(var + 1e-05)


def kernel(
    pair_hbm, mask_hbm, gl_hbm, pl_hbm, gr_hbm, pr_hbm, go_hbm, po_hbm, out_ref,
    mask_ref, pair_v, w_v, msg, fac, prod, prods, pairs, mx, my, mask_v, s8, s4, gate_v,
    load_sem, mask_load_sem, wload_sem, send_sem, fac_sem, prods_sem, pairs_sem, mask_sem,
):
    me = lax.axis_index("axial")
    z, y = lax.div(me, 64), lax.rem(lax.div(me, 8), 8)
    x, c = lax.rem(lax.div(me, 2), 4), lax.rem(me, 2)
    zt = [64 * lax.rem(z + k, 2) for k in range(NZ)]
    yt = [8 * lax.rem(y + k, 8) for k in range(NY)]
    xt = [2 * lax.rem(x + k, 4) for k in range(NX)]
    ct = [lax.rem(c + k, 2) for k in range(NC)]
    targets = [zt[dz] + yt[dy] + xt[dx] + ct[dc] for dz, dy, dx, dc in PEERS]

    barrier = pltpu.get_barrier_semaphore()
    for t in targets:
        pl.semaphore_signal(barrier, inc=1, device_id={"axial": t}, device_id_type=MESH)

    load = pltpu.make_async_copy(pair_hbm, pair_v, load_sem)
    load.start()
    mask_load = pltpu.make_async_copy(mask_hbm, mask_ref, mask_load_sem)
    mask_load.start()
    wloads = [
        pltpu.make_async_copy(ref, w_v.at[i], wload_sem.at[i])
        for i, ref in enumerate((gl_hbm, pl_hbm, gr_hbm, pr_hbm, go_hbm, po_hbm))
    ]
    for w in wloads:
        w.start()

    def send(src, dst, sem, recv_sem, t):
        pltpu.make_async_remote_copy(
            src_ref=src, dst_ref=dst, send_sem=sem, recv_sem=recv_sem,
            device_id={"axial": t}, device_id_type=MESH,
        ).start()

    def landed(ref, sem):
        pltpu.make_async_copy(ref, ref, sem).wait()

    load.wait()
    normed = layer_norm(pair_v.reshape(512, 128)[...].astype(F32), 1).astype(BF16)
    for w in wloads:
        w.wait()
    mask_load.wait()
    for f in range(2):
        gating = lax.dot_general(
            w_v[2 * f], normed, (((0,), (1,)), ((), ())), preferred_element_type=F32
        )
        values = lax.dot_general(
            w_v[2 * f + 1], normed, (((0,), (1,)), ((), ())), preferred_element_type=F32
        )
        factor = jax.nn.sigmoid(gating) * values
        for r in range(2):
            row_mask = mask_ref[r].astype(F32)
            for kh in range(2):
                q = 2 * r + kh
                s8[pl.ds(4 * f + q, 128, stride=8), :] = (
                    factor[:, 128 * q : 128 * q + 128] * row_mask
                )
    msg.reshape(1024, 128)[...] = s8[...].astype(BF16)

    k_index = lax.broadcasted_iota(jnp.int32, (2, 128), 0) * 128 + lax.broadcasted_iota(
        jnp.int32, (2, 128), 1
    )
    own_mask = jnp.where(k_index == 2 * me, mask_ref[0], 0) + jnp.where(
        k_index == 2 * me + 1, mask_ref[1], 0
    )
    xc, zy = 2 * x + c, 8 * z + y
    mx[xc] = own_mask.astype(F32)

    pl.semaphore_wait(barrier, D - 1)

    for dx, dc in itertools.product(range(NX), range(NC)):
        if dx + dc:
            t = zt[0] + yt[0] + xt[dx] + ct[dc]
            send(mx.at[xc], mx.at[xc], mask_sem.at[0], mask_sem.at[1], t)
    for t in targets[:EARLY]:
        send(msg.at[t], fac.at[me], send_sem.at[0], fac_sem, t)
    landed(mx.at[pl.ds(0, 7)], mask_sem.at[1])
    my[zy] = jnp.sum(mx[...], axis=0)
    for dy, dz in itertools.product(Y_ORDER, (1, 0)):
        if dy + dz:
            t = zt[dz] + yt[dy] + xt[0] + ct[0]
            send(my.at[zy], my.at[zy], mask_sem.at[2], mask_sem.at[3], t)
    for t in targets[EARLY:]:
        send(msg.at[t], fac.at[me], send_sem.at[0], fac_sem, t)
    pltpu.make_async_copy(msg.at[me], fac.at[me], fac_sem).start()
    for t in targets:
        send(pair_v.at[:, t], pairs.at[me], send_sem.at[1], pairs_sem, t)
    pltpu.make_async_copy(pair_v.at[:, me], pairs.at[me], pairs_sem).start()
    landed(my.at[pl.ds(0, 15)], mask_sem.at[3])
    mask_v[...] = jnp.sum(my[...], axis=0)

    landed(fac, fac_sem)
    s8[...] = fac.reshape(1024, 128)[...].astype(F32)
    halves = [s8[pl.ds(q, 128, stride=8), :] for q in range(8)]
    lefts = [
        jnp.concatenate(
            [halves[2 * r + kh] * mask_v[kh : kh + 1, :] for kh in range(2)], axis=1
        )
        for r in range(2)
    ]
    left = jnp.concatenate(lefts, axis=0).astype(BF16)
    for pz in range(NZ):
        at = slice(64 * pz, 64 * pz + 64)
        right = jnp.concatenate(
            [
                jnp.concatenate([halves[4 + 2 * r + kh][at] for kh in range(2)], axis=1)
                for r in range(2)
            ],
            axis=0,
        ).astype(BF16)
        product = lax.dot_general(right, left, NT, preferred_element_type=F32)
        for rj, ri in itertools.product(range(2), range(2)):
            s4[pl.ds(256 * pz + 2 * rj + ri, 64, stride=4), :] = product[
                64 * rj : 64 * rj + 64, 128 * ri : 128 * ri + 128
            ]
        prod.at[pl.ds(64 * pz, 64)].reshape(256, 128)[...] = s4[
            pl.ds(256 * pz, 256), :
        ].astype(BF16)
        for py, dx, dc in itertools.product((0, 1, 2, 3, 7, 6, 5, 4), X_ORDER, (1, 0)):
            t = 64 * pz + 8 * py + xt[dx] + ct[dc]

            def send_prod(t=t):
                send(prod.at[t], prods.at[me], send_sem.at[2], prods_sem, t)

            if dx + dc:
                send_prod()
            else:
                pl.when(t != me)(send_prod)
    pltpu.make_async_copy(prod.at[me], prods.at[me], prods_sem).start()

    landed(pairs, pairs_sem)
    columns = pairs.reshape(512, 128)
    normed = layer_norm(columns[...].astype(F32), 1).astype(BF16)
    gate_v[...] = jax.nn.sigmoid(
        jnp.dot(normed, w_v[4], preferred_element_type=F32)
    )

    landed(prods, prods_sem)
    s4[...] = prods.reshape(512, 128)[...].astype(F32)
    update = []
    for rj, ri in itertools.product(range(2), range(2)):
        channels = s4[pl.ds(2 * rj + ri, 128, stride=4), :]
        update.append(
            lax.dot_general(
                layer_norm(channels, 0).astype(BF16), w_v[5], TN, preferred_element_type=F32
            )
        )
    for (rj, ri), part in zip(itertools.product(range(2), range(2)), update):
        s4[pl.ds(2 * ri + rj, 128, stride=4), :] = part
    out_ref[...] = (columns[...].astype(F32) + gate_v[...] * s4[...]).astype(BF16)

    landed(msg.at[pl.ds(0, D - 1)], send_sem.at[0])
    landed(pairs.at[pl.ds(0, D - 1)], send_sem.at[1])
    landed(prod.at[pl.ds(0, D - 1)], send_sem.at[2])
    landed(mx.at[pl.ds(0, 7)], mask_sem.at[0])
    landed(my.at[pl.ds(0, 15)], mask_sem.at[2])


def body(pair, residue_mask, *weights):
    hbm = pl.BlockSpec(memory_space=pltpu.HBM)
    inputs = [
        pltpu.with_memory_space_constraint(v, pltpu.HBM)
        for v in (pair.reshape(2, D, 2, 128), residue_mask, *weights)
    ]
    out = pl.pallas_call(
        kernel,
        out_shape=pltpu.VMEM((512, 128), BF16),
        in_specs=[hbm] * 8,
        out_specs=pl.BlockSpec(memory_space=pltpu.VMEM),
        scratch_shapes=[
            pltpu.SMEM((2,), jnp.int32),
            pltpu.VMEM((2, D, 2, 128), BF16),
            pltpu.VMEM((6, 128, 128), BF16),
            pltpu.VMEM((D, 8, 128), BF16),
            pltpu.VMEM((D, 8, 128), BF16),
            pltpu.VMEM((D, 4, 128), BF16),
            pltpu.VMEM((D, 4, 128), BF16),
            pltpu.VMEM((D, 2, 2, 128), BF16),
            pltpu.VMEM((8, 2, 128), F32),
            pltpu.VMEM((16, 2, 128), F32),
            pltpu.VMEM((2, 128), F32),
            pltpu.VMEM((1024, 128), F32),
            pltpu.VMEM((512, 128), F32),
            pltpu.VMEM((512, 128), F32),
            pltpu.SemaphoreType.DMA,
            pltpu.SemaphoreType.DMA,
            pltpu.SemaphoreType.DMA((6,)),
            pltpu.SemaphoreType.DMA((3,)),
            pltpu.SemaphoreType.DMA,
            pltpu.SemaphoreType.DMA,
            pltpu.SemaphoreType.DMA,
            pltpu.SemaphoreType.DMA((4,)),
        ],
        compiler_params=pltpu.CompilerParams(
            collective_id=0, has_side_effects=True, vmem_limit_bytes=60 << 20
        ),
    )(*inputs)
    return out.reshape(256, 2, 128)


def solution(mesh):
    return jax.shard_map(
        body,
        mesh=mesh,
        in_specs=(P(("batch", "axial"), None, None), P(("batch", "axial")))
        + (P(),) * 6,
        out_specs=P("batch", "axial", None),
        check_vma=False,
    )
```

```python
import itertools

import jax
import jax.numpy as jnp
from jax import lax
from jax.experimental import pallas as pl
from jax.experimental.pallas import tpu as pltpu
from jax.sharding import PartitionSpec as P

MESH = pl.DeviceIdType.MESH
F32, BF16 = jnp.float32, jnp.bfloat16
NZ, NY, NX, NC = 2, 8, 4, 2
D = NZ * NY * NX * NC
CH = 128
Y_ORDER = (4, 3, 5, 2, 6, 1, 7, 0)
X_ORDER = (2, 1, 3, 0)
PEERS = tuple(
    sorted(
        (d for d in itertools.product(range(NZ), range(NY), range(NX), range(NC)) if any(d)),
        key=lambda d: (
            -(d[0] + min(d[1], NY - d[1]) + min(d[2], NX - d[2])),
            -min(d[1], NY - d[1]),
            d[2],
            d[3],
            d[1],
        ),
    )
)
EARLY = 60
NT = (((1,), (1,)), ((), ()))
TN = (((0,), (0,)), ((), ()))


def layer_norm(values, axis):
    mean = jnp.mean(values, axis=axis, keepdims=True)
    centered = values - mean
    var = jnp.mean(centered * centered, axis=axis, keepdims=True)
    return centered * lax.rsqrt(var + 1e-05)


def kernel(
    pair_hbm, mask_hbm, gl_hbm, pl_hbm, gr_hbm, pr_hbm, go_hbm, po_hbm, out_ref,
    mask_ref, pair_v, w_v, msg, fac, prod, prods, pairs, mx, my, mask_v, s8, s4, gate_v,
    load_sem, mask_load_sem, wload_sem, send_sem, fac_sem, prods_sem, pairs_sem, mask_sem,
):
    me = lax.axis_index("axial")
    z, y = lax.div(me, 64), lax.rem(lax.div(me, 8), 8)
    x, c = lax.rem(lax.div(me, 2), 4), lax.rem(me, 2)
    zt = [64 * lax.rem(z + k, 2) for k in range(NZ)]
    yt = [8 * lax.rem(y + k, 8) for k in range(NY)]
    xt = [2 * lax.rem(x + k, 4) for k in range(NX)]
    ct = [lax.rem(c + k, 2) for k in range(NC)]
    targets = [zt[dz] + yt[dy] + xt[dx] + ct[dc] for dz, dy, dx, dc in PEERS]

    barrier = pltpu.get_barrier_semaphore()
    for t in targets:
        pl.semaphore_signal(barrier, inc=1, device_id={"axial": t}, device_id_type=MESH)

    load = pltpu.make_async_copy(pair_hbm, pair_v, load_sem)
    load.start()
    mask_load = pltpu.make_async_copy(mask_hbm, mask_ref, mask_load_sem)
    mask_load.start()
    wloads = [
        pltpu.make_async_copy(ref, w_v.at[i], wload_sem.at[i])
        for i, ref in enumerate((gl_hbm, pl_hbm, gr_hbm, pr_hbm, go_hbm, po_hbm))
    ]
    for w in wloads:
        w.start()

    def send(src, dst, sem, recv_sem, t):
        pltpu.make_async_remote_copy(
            src_ref=src, dst_ref=dst, send_sem=sem, recv_sem=recv_sem,
            device_id={"axial": t}, device_id_type=MESH,
        ).start()

    def landed(ref, sem):
        pltpu.make_async_copy(ref, ref, sem).wait()

    load.wait()
    normed = layer_norm(pair_v.reshape(512, 128)[...].astype(F32), 1).astype(BF16)
    for w in wloads:
        w.wait()
    mask_load.wait()
    for f in range(2):
        gating = lax.dot_general(
            w_v[2 * f], normed, (((0,), (1,)), ((), ())), preferred_element_type=F32
        )
        values = lax.dot_general(
            w_v[2 * f + 1], normed, (((0,), (1,)), ((), ())), preferred_element_type=F32
        )
        factor = jax.nn.sigmoid(gating) * values
        for r in range(2):
            row_mask = mask_ref[r].astype(F32)
            for kh in range(2):
                q = 2 * r + kh
                s8[pl.ds(4 * f + q, 128, stride=8), :] = (
                    factor[:, 128 * q : 128 * q + 128] * row_mask
                )
    msg.reshape(1024, 128)[...] = s8[...].astype(BF16)

    k_index = lax.broadcasted_iota(jnp.int32, (2, 128), 0) * 128 + lax.broadcasted_iota(
        jnp.int32, (2, 128), 1
    )
    own_mask = jnp.where(k_index == 2 * me, mask_ref[0], 0) + jnp.where(
        k_index == 2 * me + 1, mask_ref[1], 0
    )
    xc, zy = 2 * x + c, 8 * z + y
    mx[xc] = own_mask.astype(F32)

    pl.semaphore_wait(barrier, D - 1)

    for dx, dc in itertools.product(range(NX), range(NC)):
        if dx + dc:
            t = zt[0] + yt[0] + xt[dx] + ct[dc]
            send(mx.at[xc], mx.at[xc], mask_sem.at[0], mask_sem.at[1], t)
    for t in targets[:EARLY]:
        send(msg.at[t], fac.at[me], send_sem.at[0], fac_sem, t)
    landed(mx.at[pl.ds(0, 7)], mask_sem.at[1])
    my[zy] = jnp.sum(mx[...], axis=0)
    for dy, dz in itertools.product(Y_ORDER, (1, 0)):
        if dy + dz:
            t = zt[dz] + yt[dy] + xt[0] + ct[0]
            send(my.at[zy], my.at[zy], mask_sem.at[2], mask_sem.at[3], t)
    for t in targets[EARLY:]:
        send(msg.at[t], fac.at[me], send_sem.at[0], fac_sem, t)
    pltpu.make_async_copy(msg.at[me], fac.at[me], fac_sem).start()
    for py, pz in itertools.product((0, 1, 2, 3, 7, 6, 5, 4), range(NZ)):
        for dx, dc in itertools.product(X_ORDER, (1, 0)):
            t = 64 * pz + 8 * py + xt[dx] + ct[dc]

            def send_pair(t=t):
                send(pair_v.at[:, t], pairs.at[me], send_sem.at[1], pairs_sem, t)

            if dx + dc:
                send_pair()
            else:
                pl.when(t != me)(send_pair)
    pltpu.make_async_copy(pair_v.at[:, me], pairs.at[me], pairs_sem).start()
    landed(my.at[pl.ds(0, 15)], mask_sem.at[3])
    mask_v[...] = jnp.sum(my[...], axis=0)

    landed(fac, fac_sem)
    s8[...] = fac.reshape(1024, 128)[...].astype(F32)
    halves = [s8[pl.ds(q, 128, stride=8), :] for q in range(8)]
    lefts = [
        jnp.concatenate(
            [halves[2 * r + kh] * mask_v[kh : kh + 1, :] for kh in range(2)], axis=1
        )
        for r in range(2)
    ]
    left = jnp.concatenate(lefts, axis=0).astype(BF16)
    for pz in range(NZ):
        at = slice(64 * pz, 64 * pz + 64)
        right = jnp.concatenate(
            [
                jnp.concatenate([halves[4 + 2 * r + kh][at] for kh in range(2)], axis=1)
                for r in range(2)
            ],
            axis=0,
        ).astype(BF16)
        product = lax.dot_general(right, left, NT, preferred_element_type=F32)
        for rj, ri in itertools.product(range(2), range(2)):
            s4[pl.ds(256 * pz + 2 * rj + ri, 64, stride=4), :] = product[
                64 * rj : 64 * rj + 64, 128 * ri : 128 * ri + 128
            ]
        prod.at[pl.ds(64 * pz, 64)].reshape(256, 128)[...] = s4[
            pl.ds(256 * pz, 256), :
        ].astype(BF16)
        for py, dx, dc in itertools.product((0, 1, 2, 3, 7, 6, 5, 4), X_ORDER, (1, 0)):
            t = 64 * pz + 8 * py + xt[dx] + ct[dc]

            def send_prod(t=t):
                send(prod.at[t], prods.at[me], send_sem.at[2], prods_sem, t)

            if dx + dc:
                send_prod()
            else:
                pl.when(t != me)(send_prod)
    pltpu.make_async_copy(prod.at[me], prods.at[me], prods_sem).start()

    landed(pairs, pairs_sem)
    columns = pairs.reshape(512, 128)
    normed = layer_norm(columns[...].astype(F32), 1).astype(BF16)
    gate_v[...] = jax.nn.sigmoid(
        jnp.dot(normed, w_v[4], preferred_element_type=F32)
    )

    landed(prods, prods_sem)
    s4[...] = prods.reshape(512, 128)[...].astype(F32)
    update = []
    for rj, ri in itertools.product(range(2), range(2)):
        channels = s4[pl.ds(2 * rj + ri, 128, stride=4), :]
        update.append(
            lax.dot_general(
                layer_norm(channels, 0).astype(BF16), w_v[5], TN, preferred_element_type=F32
            )
        )
    for (rj, ri), part in zip(itertools.product(range(2), range(2)), update):
        s4[pl.ds(2 * ri + rj, 128, stride=4), :] = part
    out_ref[...] = (columns[...].astype(F32) + gate_v[...] * s4[...]).astype(BF16)

    landed(msg.at[pl.ds(0, D - 1)], send_sem.at[0])
    landed(pairs.at[pl.ds(0, D - 1)], send_sem.at[1])
    landed(prod.at[pl.ds(0, D - 1)], send_sem.at[2])
    landed(mx.at[pl.ds(0, 7)], mask_sem.at[0])
    landed(my.at[pl.ds(0, 15)], mask_sem.at[2])


def body(pair, residue_mask, *weights):
    hbm = pl.BlockSpec(memory_space=pltpu.HBM)
    inputs = [
        pltpu.with_memory_space_constraint(v, pltpu.HBM)
        for v in (pair.reshape(2, D, 2, 128), residue_mask, *weights)
    ]
    out = pl.pallas_call(
        kernel,
        out_shape=pltpu.VMEM((512, 128), BF16),
        in_specs=[hbm] * 8,
        out_specs=pl.BlockSpec(memory_space=pltpu.VMEM),
        scratch_shapes=[
            pltpu.SMEM((2,), jnp.int32),
            pltpu.VMEM((2, D, 2, 128), BF16),
            pltpu.VMEM((6, 128, 128), BF16),
            pltpu.VMEM((D, 8, 128), BF16),
            pltpu.VMEM((D, 8, 128), BF16),
            pltpu.VMEM((D, 4, 128), BF16),
            pltpu.VMEM((D, 4, 128), BF16),
            pltpu.VMEM((D, 2, 2, 128), BF16),
            pltpu.VMEM((8, 2, 128), F32),
            pltpu.VMEM((16, 2, 128), F32),
            pltpu.VMEM((2, 128), F32),
            pltpu.VMEM((1024, 128), F32),
            pltpu.VMEM((512, 128), F32),
            pltpu.VMEM((512, 128), F32),
            pltpu.SemaphoreType.DMA,
            pltpu.SemaphoreType.DMA,
            pltpu.SemaphoreType.DMA((6,)),
            pltpu.SemaphoreType.DMA((3,)),
            pltpu.SemaphoreType.DMA,
            pltpu.SemaphoreType.DMA,
            pltpu.SemaphoreType.DMA,
            pltpu.SemaphoreType.DMA((4,)),
        ],
        compiler_params=pltpu.CompilerParams(
            collective_id=0, has_side_effects=True, vmem_limit_bytes=60 << 20
        ),
    )(*inputs)
    return out.reshape(256, 2, 128)


def solution(mesh):
    return jax.shard_map(
        body,
        mesh=mesh,
        in_specs=(P(("batch", "axial"), None, None), P(("batch", "axial")))
        + (P(),) * 6,
        out_specs=P("batch", "axial", None),
        check_vma=False,
    )
```
